32 devices in a mesh: section: 8 (over z, x), fsdp: 4 (over y, core).
Axes of the slice: x: 2, y: 2, z: 4, core: 2. Of those that a mesh axis runs over, the one named last changes fastest.
Arguments:
- x_fwd: bfloat16 [8, 384, 4096], P('section', None, 'fsdp'), may hold values from -6 to 6
- x_saved: bfloat16 [8, 384, 4096], P('section', None, 'fsdp'), may hold values from -6 to 6
- cotangent: bfloat16 [8, 384, 4096], P('section', None, 'fsdp'), may hold values from -6 to 6
- qkv_weight: bfloat16 [8, 4096, 3, 4096], P('section', None, None, 'fsdp')
- gain: float32 [8, 4096], P('section', 'fsdp'), may hold values from 0.1 to 1.9
- block_lists: int32 [8, 3, 2], replicated, may hold values from 0 to 2, as said below
- plan: int32 [8, 2], P('section'), may hold values from 0 to 7
Outputs:
- y_next: bfloat16 [8, 384, 4096], P('section', None, 'fsdp')
- dx_prev: bfloat16 [8, 384, 4096], P('section', None, 'fsdp')
- w_grad: bfloat16 [8, 4096, 3, 4096], P('section', None, None, 'fsdp')
- gain_grad: float32 [8, 4096], P('section', 'fsdp')
The draws below stay inside these ranges and needn't reach their ends.
Inputs may be any that keep to these rules, and one draw needn't show every extreme that they name: block_lists[z, b, 0] = b; the 2 entries of a row are distinct.
All inputs are finite; a program needn't handle non-finite values.
Results may differ from the reference program's by a relative error of at most 0.024.
Values may be sent and summed in bfloat16 or wider, within the bound.
A program may use at most 128 MiB of HBM per device.

```python
import math
import jax
import jax.numpy as jnp
from jax import lax

D = 4096
HD = 128
BLK = 128
BAND = 2
SLICES = 8
TOK = 384
SECTIONS = 8
QBLOCKS = 3


def draw_qkv_weight(key, part):
    key_list = jax.random.split(key, 1)
    noise_all = jax.random.normal(key_list[0], (SECTIONS, D, 3, D), jnp.float32)
    scales = jnp.array([1.6, 1.6, 1.0], jnp.float32).reshape(1, 1, 3, 1)
    return (noise_all * scales * (1.0 / math.sqrt(D))).astype(jnp.bfloat16)


def draw_block_lists(key, part):
    column_ids = jnp.arange(QBLOCKS, dtype=jnp.int32)
    scores = jax.random.randint(key, (SLICES, QBLOCKS, QBLOCKS), 0, 4096) * QBLOCKS + column_ids[None, None, :]
    own_mask = column_ids[:, None] == column_ids[None, :]
    scores = jnp.where(own_mask[None, :, :], -1, scores)
    ranked = jnp.argsort(scores, axis=2, stable=True)
    return ranked[:, :, :BAND].astype(jnp.int32)


def draw_plan(key, part):
    key_list = jax.random.split(key, 2)
    offset = jax.random.randint(key_list[0], (), 0, SLICES)
    values = (jnp.arange(2 * SECTIONS, dtype=jnp.int32) + offset) % SLICES
    return jax.random.permutation(key_list[1], values).reshape(SECTIONS, 2).astype(jnp.int32)


def shard_levels(stream_key, shape, shards, smallest, high):
    level = 1.0
    for position, parts in shards:
        draws = jax.random.uniform(jax.random.fold_in(jax.random.fold_in(stream_key, 6), position), (parts,), jnp.float32, smallest / len(shards), high / len(shards))
        level = level * jnp.repeat(jnp.exp(draws), shape[position] // parts).reshape((-1,) + (1,) * (len(shape) - 1 - position))
    return level


def gaussian(stream_key, shape, scale, most, shards=(), held_as=jnp.bfloat16):
    values = jax.random.normal(stream_key, shape, jnp.float32) * scale
    if len(shards) > 0:
        values = shard_levels(stream_key, shape, shards, -0.22, 0.18) * values
    return jnp.clip(values, min=-most, max=most).astype(held_as)


def setup_inputs(seed: int = 0) -> dict:
    splits = jax.random.split(jax.random.key(seed), 8)
    return {
        "x_fwd": gaussian(splits[0], (SECTIONS, TOK, D), 1.0, 6.0, ((0, 8), (2, 4))),
        "x_saved": gaussian(splits[1], (SECTIONS, TOK, D), 1.0, 6.0, ((0, 8), (2, 4))),
        "cotangent": gaussian(splits[2], (SECTIONS, TOK, D), 1.0, 6.0, ((0, 8), (2, 4))),
        "qkv_weight": draw_qkv_weight(jax.random.fold_in(splits[7], 71), 0),
        "gain": jnp.clip(1.0 + 0.18 * jax.random.normal(splits[4], (SECTIONS, D), jnp.float32), 0.1, 1.9),
        "block_lists": draw_block_lists(jax.random.fold_in(splits[7], 71), 0),
        "plan": draw_plan(jax.random.fold_in(splits[7], 71), 0),
    }


EPS = 1e-05

def attend(query, key_in, value, block_ids):
    tokens, feat_width = query.shape
    head_count = feat_width // HD
    block_count = tokens // BLK
    band_size = block_ids.shape[1]
    q_blocks = query.reshape(block_count, BLK, head_count, HD)
    k_rows = key_in.reshape(block_count, BLK, head_count, HD)[block_ids].reshape(block_count, band_size * BLK, head_count, HD)
    v_rows = value.reshape(block_count, BLK, head_count, HD)[block_ids].reshape(block_count, band_size * BLK, head_count, HD)
    scores = jnp.einsum('qthd,qshd->qhts', q_blocks.astype(jnp.float32), k_rows.astype(jnp.float32)) * (1.0 / math.sqrt(HD))
    row_max = lax.optimization_barrier(jnp.max(scores, axis=3, keepdims=True))
    expd = jnp.exp(scores - row_max)
    probs = expd / lax.optimization_barrier(jnp.sum(expd, axis=3, keepdims=True))
    probs_low = probs.astype(jnp.bfloat16)
    output = jnp.einsum('qhts,qshd->qthd', probs_low.astype(jnp.float32), v_rows.astype(jnp.float32)).reshape(tokens, feat_width)
    return (output, (probs, probs_low, q_blocks, k_rows, v_rows))

def attend_back(upstream, block_ids, saved):
    probs, probs_low, q_blocks, k_rows, v_rows = saved
    block_count, block_len, head_count, head_size = q_blocks.shape
    band_size = block_ids.shape[1]
    tokens = block_count * block_len
    c_blocks = upstream.reshape(block_count, block_len, head_count, head_size).astype(jnp.float32)
    grad_vrows = jnp.einsum('qhts,qthd->qshd', probs_low.astype(jnp.float32), c_blocks)
    grad_p = jnp.einsum('qthd,qshd->qhts', c_blocks, v_rows.astype(jnp.float32))
    grad_s = probs * (grad_p - lax.optimization_barrier(jnp.sum(probs * grad_p, axis=3, keepdims=True))) * (1.0 / math.sqrt(HD))
    grad_s_low = grad_s.astype(jnp.bfloat16)
    grad_q = jnp.einsum('qhts,qshd->qthd', grad_s_low.astype(jnp.float32), k_rows.astype(jnp.float32))
    grad_krows = jnp.einsum('qhts,qthd->qshd', grad_s_low.astype(jnp.float32), q_blocks.astype(jnp.float32))
    onehot = (block_ids[:, :, None] == jnp.arange(block_count, dtype=jnp.int32)[None, None, :]).astype(jnp.float32)
    band_shape = (block_count, band_size, block_len, head_count, head_size)
    grad_k = jnp.einsum('qbk,qbthd->kthd', onehot, grad_krows.reshape(band_shape))
    grad_v = jnp.einsum('qbk,qbthd->kthd', onehot, grad_vrows.reshape(band_shape))
    return (grad_q.reshape(tokens, -1), grad_k.reshape(tokens, -1), grad_v.reshape(tokens, -1))

def project(x_in, gain_row, w_flat):
    x_wide = x_in.astype(jnp.float32)
    row_scale = lax.rsqrt(lax.optimization_barrier(jnp.mean(x_wide * x_wide, axis=1)) + EPS)
    scaled_in = (x_wide * gain_row[None, :]).astype(jnp.bfloat16)
    product = jnp.dot(scaled_in, w_flat, preferred_element_type=jnp.float32)
    projected = (row_scale[:, None] * product).astype(jnp.bfloat16)
    return (x_wide, row_scale, scaled_in, projected)

def reference(x_fwd, x_saved, cotangent, qkv_weight, gain, block_lists, plan):

    def section_step(section_args):
        forward_in, saved_in, upstream, weight, gain_row, sched_row = section_args
        w_flat = weight.reshape(D, 3 * D)
        tokens = forward_in.shape[0]
        wide_fwd, scale_fwd, scaled_fwd, proj_fwd = project(forward_in, gain_row, w_flat)
        lists_fwd = block_lists[sched_row[0]]
        attn_fwd = attend(proj_fwd[:, :D], proj_fwd[:, D:2 * D], proj_fwd[:, 2 * D:], lists_fwd)[0]
        result = (wide_fwd + attn_fwd).astype(jnp.bfloat16)
        wide_bwd, scale_bwd, scaled_bwd, proj_bwd = project(saved_in, gain_row, w_flat)
        lists_bwd = block_lists[sched_row[1]]
        saved = attend(proj_bwd[:, :D], proj_bwd[:, D:2 * D], proj_bwd[:, 2 * D:], lists_bwd)[1]
        grad_q, grad_k, grad_v = attend_back(upstream, lists_bwd, saved)
        stacked = jnp.stack([grad_q, grad_k, grad_v], axis=1).reshape(tokens, 3 * D)
        grads = (scale_bwd[:, None] * stacked).astype(jnp.bfloat16)
        grad_w = lax.dot_general(scaled_bwd, grads, (((0,), (0,)), ((), ())), preferred_element_type=jnp.float32)
        grad_w = grad_w.astype(jnp.bfloat16).reshape(D, 3, D)
        grad_in = lax.dot_general(grads, w_flat, (((1,), (1,)), ((), ())), preferred_element_type=jnp.float32)
        row_total = lax.optimization_barrier(jnp.sum(scaled_bwd.astype(jnp.float32) * grad_in, axis=1))
        grad_x = upstream.astype(jnp.float32) + gain_row[None, :] * grad_in
        grad_x = grad_x - (scale_bwd * scale_bwd * row_total / D)[:, None] * wide_bwd
        grad_gain = lax.optimization_barrier(jnp.sum(wide_bwd * grad_in, axis=0))
        return (result, grad_x.astype(jnp.bfloat16), grad_w, grad_gain)
    results, grad_xs, grad_ws, grad_gains = lax.map(section_step, (x_fwd, x_saved, cotangent, qkv_weight, gain, plan))
    return (jnp.roll(results, 1, axis=0), jnp.roll(grad_xs, -1, axis=0), grad_ws, grad_gains)
```

```python
import math

import jax
import jax.numpy as jnp
from jax import lax
from jax.experimental import pallas as pl
from jax.experimental.pallas import tpu as pltpu
from jax.sharding import PartitionSpec as P

HD = 128
BLK = 128
EPS = 1e-05
INV = 1.0 / math.sqrt(HD)
VMEM = 40 * 1024 * 1024
F32 = jnp.float32
BF16 = jnp.bfloat16
NT = (((1,), (1,)), ((), ()))
TN = (((0,), (0,)), ((), ()))


def params(*sem):
    return pltpu.CompilerParams(dimension_semantics=sem, vmem_limit_bytes=VMEM)


def project_body(x_ref, w_ref, scale_ref, out_ref):
    product = jnp.dot(x_ref[...], w_ref[0], preferred_element_type=F32)
    out_ref[0] = (scale_ref[...] * product).astype(BF16)


def project(x, w3, scale):
    tokens, width = x.shape
    local = w3.shape[2]
    nt = min(256, local)
    return pl.pallas_call(
        project_body,
        grid=(3, local // nt),
        in_specs=[
            pl.BlockSpec((tokens, width), lambda k, j: (0, 0)),
            pl.BlockSpec((1, width, nt), lambda k, j: (k, 0, j)),
            pl.BlockSpec((tokens, 1), lambda k, j: (0, 0)),
        ],
        out_specs=pl.BlockSpec((1, tokens, nt), lambda k, j: (k, 0, j)),
        out_shape=jax.ShapeDtypeStruct((3, tokens, local), BF16),
        compiler_params=params("arbitrary", "arbitrary"),
        cost_estimate=pl.CostEstimate(
            flops=6 * tokens * width * local, bytes_accessed=6 * width * local, transcendentals=0
        ),
    )(x, w3, scale)


def probs_of(q_b, key, allowed):
    scores = lax.dot_general(q_b, key, NT, preferred_element_type=F32) * INV
    scores = jnp.where(allowed > 0.0, scores, -jnp.inf)
    expd = jnp.exp(scores - jnp.max(scores, axis=1, keepdims=True))
    return expd * (1.0 / jnp.sum(expd, axis=1, keepdims=True))


def forward_body(allow_ref, q_ref, k_ref, v_ref, x_ref, out_ref):
    tokens, cols = x_ref.shape
    for h in range(cols // HD):
        hs = slice(h * HD, (h + 1) * HD)
        key, value = k_ref[0, :, hs], v_ref[0, :, hs]
        for b in range(tokens // BLK):
            bs = slice(b * BLK, (b + 1) * BLK)
            low = probs_of(q_ref[0, bs, hs], key, allow_ref[b : b + 1, :]).astype(BF16)
            attn = jnp.dot(low, value, preferred_element_type=F32)
            out_ref[bs, hs] = (x_ref[bs, hs].astype(F32) + attn).astype(BF16)


def backward_body(allow_ref, q_ref, k_ref, v_ref, c_ref, scale_ref, grads_ref, total_ref):
    tokens, cols = c_ref.shape

    @pl.when(pl.program_id(0) == 0)
    def _():
        total_ref[...] = jnp.zeros_like(total_ref)

    for h in range(cols // HD):
        hs = slice(h * HD, (h + 1) * HD)
        key, value = k_ref[0, :, hs], v_ref[0, :, hs]
        grad_k = jnp.zeros((tokens, HD), F32)
        grad_v = jnp.zeros((tokens, HD), F32)
        for b in range(tokens // BLK):
            bs = slice(b * BLK, (b + 1) * BLK)
            q_b, c_b = q_ref[0, bs, hs], c_ref[bs, hs]
            probs = probs_of(q_b, key, allow_ref[b : b + 1, :])
            grad_v += lax.dot_general(probs.astype(BF16), c_b, TN, preferred_element_type=F32)
            grad_p = lax.dot_general(c_b, value, NT, preferred_element_type=F32)
            inner = jnp.sum(probs * grad_p, axis=1, keepdims=True)
            low = (probs * (grad_p - inner) * INV).astype(BF16)
            grad_k += lax.dot_general(low, q_b, TN, preferred_element_type=F32)
            grad_q = scale_ref[bs, :] * jnp.dot(low, key, preferred_element_type=F32)
            grad_q = grad_q.astype(BF16)
            grads_ref[0, bs, hs] = grad_q
            total_ref[bs, :] += grad_q.astype(F32) * q_b.astype(F32)
        grad_k = (scale_ref[...] * grad_k).astype(BF16)
        grad_v = (scale_ref[...] * grad_v).astype(BF16)
        grads_ref[1, :, hs] = grad_k
        grads_ref[2, :, hs] = grad_v
        total_ref[...] += grad_k.astype(F32) * key.astype(F32) + grad_v.astype(F32) * value.astype(F32)


def attention_specs(tokens, hw):
    part = lambda k: pl.BlockSpec((1, tokens, hw), lambda h: (k, 0, h))
    return [
        pl.BlockSpec((tokens // BLK, tokens), lambda h: (0, 0)),
        part(0),
        part(1),
        part(2),
        pl.BlockSpec((tokens, hw), lambda h: (0, h)),
    ]


def attend_forward(allowed, proj, x):
    tokens, local = x.shape
    hw = min(2 * HD, local)
    return pl.pallas_call(
        forward_body,
        grid=(local // hw,),
        in_specs=attention_specs(tokens, hw),
        out_specs=pl.BlockSpec((tokens, hw), lambda h: (0, h)),
        out_shape=jax.ShapeDtypeStruct((tokens, local), BF16),
        compiler_params=params("arbitrary"),
        cost_estimate=pl.CostEstimate(
            flops=16 * tokens * tokens * local, bytes_accessed=10 * tokens * local, transcendentals=0
        ),
    )(allowed, proj, proj, proj, x)


def attend_backward(allowed, proj, c, scale):
    tokens, local = c.shape
    hw = min(2 * HD, local)
    return pl.pallas_call(
        backward_body,
        grid=(local // hw,),
        in_specs=attention_specs(tokens, hw) + [pl.BlockSpec((tokens, 1), lambda h: (0, 0))],
        out_specs=[
            pl.BlockSpec((3, tokens, hw), lambda h: (0, 0, h)),
            pl.BlockSpec((tokens, HD), lambda h: (0, 0)),
        ],
        out_shape=[
            jax.ShapeDtypeStruct((3, tokens, local), BF16),
            jax.ShapeDtypeStruct((tokens, HD), F32),
        ],
        compiler_params=params("arbitrary"),
        cost_estimate=pl.CostEstimate(
            flops=40 * tokens * tokens * local, bytes_accessed=14 * tokens * local, transcendentals=0
        ),
    )(allowed, proj, proj, proj, c, scale)


def grad_in_body(ids_ref, grads_ref, w_ref, out_ref):
    total = lax.dot_general(grads_ref[0], w_ref[0], NT, preferred_element_type=F32)
    for k in (1, 2):
        total += lax.dot_general(grads_ref[k], w_ref[k], NT, preferred_element_type=F32)
    out_ref[0] = total.astype(out_ref.dtype)


def grad_in_blocks(ids, grads, w3, out_type):
    tokens, local = grads.shape[1:]
    count = ids.shape[0]
    ft = min(512, local)
    steps = local // ft
    return pl.pallas_call(
        grad_in_body,
        grid_spec=pltpu.PrefetchScalarGridSpec(
            num_scalar_prefetch=1,
            grid=(count, steps),
            in_specs=[
                pl.BlockSpec((3, tokens, local), lambda i, j, ids: (0, 0, 0)),
                pl.BlockSpec((3, ft, local), lambda i, j, ids: (0, ids[i] * steps + j, 0)),
            ],
            out_specs=pl.BlockSpec((1, tokens, ft), lambda i, j, ids: (i, 0, j)),
        ),
        out_shape=jax.ShapeDtypeStruct((count, tokens, local), out_type),
        compiler_params=params("arbitrary", "arbitrary"),
        cost_estimate=pl.CostEstimate(
            flops=6 * tokens * count * local * local,
            bytes_accessed=6 * count * local * local,
            transcendentals=0,
        ),
    )(ids, grads, w3)


def grad_w_body(x_ref, grads_ref, out_ref):
    flipped = x_ref[...].T
    for k in range(3):
        out_ref[k] = jnp.dot(flipped, grads_ref[k], preferred_element_type=F32).astype(BF16)


def grad_weight(x, grads):
    tokens, width = x.shape
    local = grads.shape[2]
    ft = 512
    return pl.pallas_call(
        grad_w_body,
        grid=(width // ft,),
        in_specs=[
            pl.BlockSpec((tokens, ft), lambda j: (0, j)),
            pl.BlockSpec((3, tokens, local), lambda j: (0, 0, 0)),
        ],
        out_specs=pl.BlockSpec((3, ft, local), lambda j: (0, j, 0)),
        out_shape=jax.ShapeDtypeStruct((3, width, local), BF16),
        compiler_params=params("arbitrary"),
        cost_estimate=pl.CostEstimate(
            flops=6 * tokens * width * local, bytes_accessed=6 * width * local, transcendentals=0
        ),
    )(x, grads)


def shifted(block, axis, distance):
    n = lax.axis_size(axis)
    return lax.ppermute(block, axis, [((i - distance) % n, i) for i in range(n)])


def allowed_keys(ids, tokens):
    blocks = jnp.arange(tokens, dtype=jnp.int32) // BLK
    return jnp.any(ids[:, :, None] == blocks[None, None, :], axis=1).astype(F32)


def on_device(x_fwd, x_saved, cotangent, qkv_weight, gain, block_lists, plan):
    forward_in, saved_in, upstream = x_fwd[0], x_saved[0], cotangent[0]
    gain_row = gain[0][None, :]
    w3 = jnp.transpose(qkv_weight[0], (1, 0, 2))
    full_width, local = w3.shape[1:]
    tokens = forward_in.shape[0]
    n = lax.axis_size("fsdp")
    chips = n // 2
    me = lax.axis_index("fsdp")
    chip, core = me // 2, me % 2

    wide_fwd = forward_in.astype(F32)
    wide_bwd = saved_in.astype(F32)
    scaled_bwd = (wide_bwd * gain_row).astype(BF16)
    scaled_fwd = (wide_fwd * gain_row).astype(BF16)
    squares = jnp.stack([jnp.sum(wide_fwd * wide_fwd, axis=1), jnp.sum(wide_bwd * wide_bwd, axis=1)])
    whole_bwd = lax.all_gather(scaled_bwd, "fsdp", axis=1, tiled=True)
    squares = jnp.sum(lax.all_gather(squares, "fsdp"), axis=0)
    whole_fwd = lax.all_gather(scaled_fwd, "fsdp", axis=1, tiled=True)
    scales = lax.rsqrt(squares / full_width + EPS)
    scale_fwd, scale_bwd = scales[0][:, None], scales[1][:, None]

    proj_bwd = project(whole_bwd, w3, scale_bwd)
    allowed_bwd = allowed_keys(block_lists[plan[0, 1]], tokens)
    grads, totals = attend_backward(allowed_bwd, proj_bwd, upstream, scale_bwd)
    totals = jnp.sum(lax.all_gather(jnp.sum(totals, axis=1), "fsdp"), axis=0)

    others = jnp.arange(chips, dtype=jnp.int32)
    theirs = grad_in_blocks(others * 2 + 1 - core, grads, w3, BF16)
    from_core = lax.ppermute(theirs, "fsdp", [(i, i ^ 1) for i in range(n)])
    far = (chip + 1 + jnp.arange(chips - 1, dtype=jnp.int32)) % chips
    far_part = grad_in_blocks(far * 2 + core, grads, w3, F32)
    arrived = []
    for d in range(1, chips):
        here = lax.dynamic_index_in_dim(from_core, (chip + d) % chips, 0, keepdims=False)
        send = (far_part[d - 1] + here.astype(F32)).astype(BF16)
        route = [(i, ((i // 2 + d) % chips) * 2 + i % 2) for i in range(n)]
        arrived.append(lax.ppermute(send, "fsdp", route))
    own_in = grad_in_blocks(me[None].astype(jnp.int32), grads, w3, F32)[0]
    own_in += lax.dynamic_index_in_dim(from_core, chip, 0, keepdims=False).astype(F32)

    proj_fwd = project(whole_fwd, w3, scale_fwd)
    allowed_fwd = allowed_keys(block_lists[plan[0, 0]], tokens)
    result = attend_forward(allowed_fwd, proj_fwd, forward_in)
    sent_on = shifted(result[None], "section", 1)

    for block in arrived:
        own_in += block.astype(F32)
    grad_x = upstream.astype(F32) + gain_row * own_in
    grad_x = grad_x - scale_bwd * (totals / full_width)[:, None] * wide_bwd
    sent_back = shifted(grad_x.astype(BF16)[None], "section", -1)
    grad_gain = jnp.sum(wide_bwd * own_in, axis=0)[None]
    grad_w = jnp.transpose(grad_weight(whole_bwd, grads), (1, 0, 2))[None]
    return (sent_on, sent_back, grad_w, grad_gain)


def solution(mesh):
    in_specs = (
        P("section", None, "fsdp"),
        P("section", None, "fsdp"),
        P("section", None, "fsdp"),
        P("section", None, None, "fsdp"),
        P("section", "fsdp"),
        P(),
        P("section", None),
    )
    out_specs = (
        P("section", None, "fsdp"),
        P("section", None, "fsdp"),
        P("section", None, None, "fsdp"),
        P("section", "fsdp"),
    )
    return jax.shard_map(
        on_device, mesh=mesh, in_specs=in_specs, out_specs=out_specs, check_vma=False
    )
```

```python
import math

import jax
import jax.numpy as jnp
from jax import lax
from jax.experimental import pallas as pl
from jax.experimental.pallas import tpu as pltpu
from jax.sharding import PartitionSpec as P

HD = 128
BLK = 128
EPS = 1e-05
INV = 1.0 / math.sqrt(HD)
LOG2E = math.log2(math.e)
VMEM = 40 * 1024 * 1024
F32 = jnp.float32
BF16 = jnp.bfloat16
NT = (((1,), (1,)), ((), ()))
TN = (((0,), (0,)), ((), ()))


def cost(flops, moved):
    return pl.CostEstimate(flops=flops // 16, bytes_accessed=moved // 16, transcendentals=0)


def params(*sem):
    return pltpu.CompilerParams(dimension_semantics=sem, vmem_limit_bytes=VMEM)


def total_of(x_refs, w_refs):
    total = jnp.dot(x_refs[0][...], w_refs[0][0], preferred_element_type=F32)
    for x_ref, w_ref in zip(x_refs[1:], w_refs[1:]):
        total += jnp.dot(x_ref[...], w_ref[0], preferred_element_type=F32)
    return total


def near_body(ids_ref, *refs):
    count = (len(refs) - 1) // 2
    refs[-1][0] = total_of(refs[:count], refs[count:-1])


def far_body(ids_ref, *refs):
    acc_ref, scale_ref, out_ref = refs[-3:]
    count = (len(refs) - 3) // 2
    product = acc_ref[0] + total_of(refs[:count], refs[count:-3])
    out_ref[0] = (scale_ref[...] * product).astype(BF16)


def operand_specs(count, tokens, local, nt):
    specs = [pl.BlockSpec((tokens, local), lambda k, j, ids: (0, 0)) for _ in range(count)]
    for i in range(count):
        specs.append(pl.BlockSpec((1, local, nt), lambda k, j, ids, i=i: (k, ids[i], j)))
    return specs


def project_cost(tokens, count, local):
    return cost(6 * tokens * count * local * local, 6 * count * local * local)


def project_near(ids, blocks, w3):
    tokens, local = blocks[0].shape
    nt = min(256, local)
    count = len(blocks)
    return pl.pallas_call(
        near_body,
        grid_spec=pltpu.PrefetchScalarGridSpec(
            num_scalar_prefetch=1,
            grid=(3, local // nt),
            in_specs=operand_specs(count, tokens, local, nt),
            out_specs=pl.BlockSpec((1, tokens, nt), lambda k, j, ids: (k, 0, j)),
        ),
        out_shape=jax.ShapeDtypeStruct((3, tokens, local), F32),
        compiler_params=params("arbitrary", "arbitrary"),
        cost_estimate=project_cost(tokens, count, local),
    )(ids, *blocks, *[w3] * count)


def project_far(ids, blocks, w3, acc, half, scale):
    tokens, local = blocks[0].shape
    nt = min(256, local)
    count = len(blocks)
    return pl.pallas_call(
        far_body,
        grid_spec=pltpu.PrefetchScalarGridSpec(
            num_scalar_prefetch=1,
            grid=(3, local // nt),
            in_specs=operand_specs(count, tokens, local, nt)
            + [
                pl.BlockSpec((1, tokens, nt), lambda k, j, ids: (k, half, j)),
                pl.BlockSpec((tokens, 1), lambda k, j, ids: (0, 0)),
            ],
            out_specs=pl.BlockSpec((1, tokens, nt), lambda k, j, ids: (k, 0, j)),
        ),
        out_shape=jax.ShapeDtypeStruct((3, tokens, local), BF16),
        compiler_params=params("arbitrary", "arbitrary"),
        cost_estimate=project_cost(tokens, count, local),
    )(ids, *blocks, *[w3] * count, acc, scale)


def probs_of(q_b, key_a, key_b):
    s_a = lax.dot_general(key_a, q_b, NT, preferred_element_type=F32)
    s_b = lax.dot_general(key_b, q_b, NT, preferred_element_type=F32)
    top = jnp.max(jnp.maximum(s_a, s_b), axis=0, keepdims=True)
    e_a = jnp.exp2((s_a - top) * (INV * LOG2E))
    e_b = jnp.exp2((s_b - top) * (INV * LOG2E))
    share = 1.0 / jnp.sum(e_a + e_b, axis=0, keepdims=True)
    return e_a * share, e_b * share


def other_rows(ids_ref, b):
    return pl.ds(pl.multiple_of(ids_ref[b, 1] * BLK, BLK), BLK)


def forward_body(ids_ref, q_ref, k_ref, v_ref, x_ref, out_ref):
    tokens, cols = x_ref.shape
    for h in range(cols // HD):
        hs = slice(h * HD, (h + 1) * HD)
        for b in range(tokens // BLK):
            bs = slice(b * BLK, (b + 1) * BLK)
            other = other_rows(ids_ref, b)
            p_a, p_b = probs_of(q_ref[0, bs, hs], k_ref[0, bs, hs], k_ref[0, other, hs])
            attn = lax.dot_general(p_a.astype(BF16), v_ref[0, bs, hs], TN, preferred_element_type=F32)
            attn += lax.dot_general(
                p_b.astype(BF16), v_ref[0, other, hs], TN, preferred_element_type=F32
            )
            out_ref[bs, hs] = (x_ref[bs, hs].astype(F32) + attn).astype(BF16)


def backward_body(ids_ref, q_ref, k_ref, v_ref, c_ref, scale_ref, grads_ref, total_ref, gk_ref, gv_ref):
    tokens, cols = c_ref.shape

    @pl.when(pl.program_id(0) == 0)
    def _():
        total_ref[...] = jnp.zeros_like(total_ref)

    for h in range(cols // HD):
        hs = slice(h * HD, (h + 1) * HD)
        later = []
        for b in range(tokens // BLK):
            bs = slice(b * BLK, (b + 1) * BLK)
            other = other_rows(ids_ref, b)
            q_b, c_b = q_ref[0, bs, hs], c_ref[bs, hs]
            key_a, key_b = k_ref[0, bs, hs], k_ref[0, other, hs]
            p_a, p_b = probs_of(q_b, key_a, key_b)
            gp_a = lax.dot_general(v_ref[0, bs, hs], c_b, NT, preferred_element_type=F32)
            gp_b = lax.dot_general(v_ref[0, other, hs], c_b, NT, preferred_element_type=F32)
            inner = jnp.sum(p_a * gp_a + p_b * gp_b, axis=0, keepdims=True)
            gs_a = (p_a * (gp_a - inner) * INV).astype(BF16)
            gs_b = (p_b * (gp_b - inner) * INV).astype(BF16)
            gv_ref[h, bs, :] = jnp.dot(p_a.astype(BF16), c_b, preferred_element_type=F32)
            gk_ref[h, bs, :] = jnp.dot(gs_a, q_b, preferred_element_type=F32)
            later.append((other, p_b.astype(BF16), c_b, gs_b, q_b))
            grad_q = lax.dot_general(gs_a, key_a, TN, preferred_element_type=F32)
            grad_q += lax.dot_general(gs_b, key_b, TN, preferred_element_type=F32)
            grad_q = (scale_ref[bs, :] * grad_q).astype(BF16)
            grads_ref[0, bs, hs] = grad_q
            total_ref[bs, :] += grad_q.astype(F32) * q_b.astype(F32)
        for other, p_b, c_b, gs_b, q_b in later:
            gv_ref[h, other, :] += jnp.dot(p_b, c_b, preferred_element_type=F32)
            gk_ref[h, other, :] += jnp.dot(gs_b, q_b, preferred_element_type=F32)
        grad_k = (scale_ref[...] * gk_ref[h]).astype(BF16)
        grad_v = (scale_ref[...] * gv_ref[h]).astype(BF16)
        grads_ref[1, :, hs] = grad_k
        grads_ref[2, :, hs] = grad_v
        total_ref[...] += grad_k.astype(F32) * k_ref[0, :, hs].astype(F32)
        total_ref[...] += grad_v.astype(F32) * v_ref[0, :, hs].astype(F32)


def attention_specs(tokens, hw):
    part = lambda k: pl.BlockSpec((1, tokens, hw), lambda h, ids: (k, 0, h))
    return [part(0), part(1), part(2), pl.BlockSpec((tokens, hw), lambda h, ids: (0, h))]


def attend_forward(ids, proj, x):
    tokens, local = x.shape
    hw = min(2 * HD, local)
    return pl.pallas_call(
        forward_body,
        grid_spec=pltpu.PrefetchScalarGridSpec(
            num_scalar_prefetch=1,
            grid=(local // hw,),
            in_specs=attention_specs(tokens, hw),
            out_specs=pl.BlockSpec((tokens, hw), lambda h, ids: (0, h)),
        ),
        out_shape=jax.ShapeDtypeStruct((tokens, local), BF16),
        compiler_params=params("arbitrary"),
        cost_estimate=cost(12 * tokens * tokens * local, 10 * tokens * local),
    )(ids, proj, proj, proj, x)


def attend_backward(ids, proj, c, scale):
    tokens, local = c.shape
    hw = min(2 * HD, local)
    return pl.pallas_call(
        backward_body,
        grid_spec=pltpu.PrefetchScalarGridSpec(
            num_scalar_prefetch=1,
            grid=(local // hw,),
            in_specs=attention_specs(tokens, hw)
            + [pl.BlockSpec((tokens, 1), lambda h, ids: (0, 0))],
            out_specs=[
                pl.BlockSpec((3, tokens, hw), lambda h, ids: (0, 0, h)),
                pl.BlockSpec((tokens, HD), lambda h, ids: (0, 0)),
            ],
            scratch_shapes=[pltpu.VMEM((hw // HD, tokens, HD), F32) for _ in range(2)],
        ),
        out_shape=[
            jax.ShapeDtypeStruct((3, tokens, local), BF16),
            jax.ShapeDtypeStruct((tokens, HD), F32),
        ],
        compiler_params=params("arbitrary"),
        cost_estimate=cost(24 * tokens * tokens * local, 14 * tokens * local),
    )(ids, proj, proj, proj, c, scale)


def grad_in_body(ids_ref, grads_ref, w_ref, out_ref):
    total = lax.dot_general(grads_ref[0], w_ref[0], NT, preferred_element_type=F32)
    for k in (1, 2):
        total += lax.dot_general(grads_ref[k], w_ref[k], NT, preferred_element_type=F32)
    out_ref[0] = total.astype(out_ref.dtype)


def grad_in_blocks(ids, grads, w3, out_type):
    tokens, local = grads.shape[1:]
    count = ids.shape[0]
    ft = min(512, local)
    steps = local // ft
    return pl.pallas_call(
        grad_in_body,
        grid_spec=pltpu.PrefetchScalarGridSpec(
            num_scalar_prefetch=1,
            grid=(count, steps),
            in_specs=[
                pl.BlockSpec((3, tokens, local), lambda i, j, ids: (0, 0, 0)),
                pl.BlockSpec((3, ft, local), lambda i, j, ids: (0, ids[i] * steps + j, 0)),
            ],
            out_specs=pl.BlockSpec((1, tokens, ft), lambda i, j, ids: (i, 0, j)),
        ),
        out_shape=jax.ShapeDtypeStruct((count, tokens, local), out_type),
        compiler_params=params("arbitrary", "arbitrary"),
        cost_estimate=cost(6 * tokens * count * local * local, 6 * count * local * local),
    )(ids, grads, w3)


def grad_w_body(ids_ref, *refs):
    grads_ref, out_ref = refs[-2:]
    for i, x_ref in enumerate(refs[:-2]):

        @pl.when(pl.program_id(0) == i)
        def _():
            ft = out_ref.shape[1]
            start = pl.multiple_of(pl.program_id(1) * ft, ft)
            flipped = x_ref[:, pl.ds(start, ft)].T
            for k in range(3):
                out = jnp.dot(flipped, grads_ref[k], preferred_element_type=F32)
                out_ref[k] = out.astype(BF16)


def grad_weight(ids, blocks, grads):
    _, tokens, local = grads.shape
    count = len(blocks)
    ft = min(1024, local)
    steps = local // ft
    return pl.pallas_call(
        grad_w_body,
        grid_spec=pltpu.PrefetchScalarGridSpec(
            num_scalar_prefetch=1,
            grid=(count, steps),
            in_specs=[pl.BlockSpec((tokens, local), lambda i, j, ids: (0, 0)) for _ in blocks]
            + [pl.BlockSpec((3, tokens, local), lambda i, j, ids: (0, 0, 0))],
            out_specs=pl.BlockSpec((3, ft, local), lambda i, j, ids: (0, ids[i] * steps + j, 0)),
        ),
        out_shape=jax.ShapeDtypeStruct((3, count * local, local), BF16),
        compiler_params=params("arbitrary", "arbitrary"),
        cost_estimate=project_cost(tokens, count, local),
    )(ids, *blocks, grads)


def shifted(block, axis, distance):
    n = lax.axis_size(axis)
    return lax.ppermute(block, axis, [((i - distance) % n, i) for i in range(n)])


def swap_core(block):
    return lax.ppermute(block, "fsdp", [(i, i ^ 1) for i in range(lax.axis_size("fsdp"))])


def next_chip(block, distance):
    n = lax.axis_size("fsdp")
    route = [(i, ((i // 2 + distance) % (n // 2)) * 2 + i % 2) for i in range(n)]
    return lax.ppermute(block, "fsdp", route)


def summed(block):
    total = block
    for distance in range(1, lax.axis_size("fsdp")):
        total += shifted(block, "fsdp", distance)
    return total


def on_device(x_fwd, x_saved, cotangent, qkv_weight, gain, block_lists, plan):
    forward_in, saved_in, upstream = x_fwd[0], x_saved[0], cotangent[0]
    gain_row = gain[0][None, :]
    w3 = jnp.transpose(qkv_weight[0], (1, 0, 2))
    full_width, local = w3.shape[1:]
    tokens = forward_in.shape[0]
    n = lax.axis_size("fsdp")
    chips = n // 2
    me = lax.axis_index("fsdp").astype(jnp.int32)
    chip, core = lax.shift_right_logical(me, 1), me & 1
    wrap = lambda c: jnp.where(c < 0, c + chips, jnp.where(c >= chips, c - chips, c))
    near_ids = jnp.stack([me, me ^ 1])
    source = [wrap(chip - d) * 2 + core for d in range(1, chips)]
    far_ids = jnp.stack([i for s in source for i in (s, s ^ 1)])

    wide_fwd = forward_in.astype(F32)
    wide_bwd = saved_in.astype(F32)
    scaled_bwd = (wide_bwd * gain_row).astype(BF16)
    scaled_fwd = (wide_fwd * gain_row).astype(BF16)
    squares = jnp.stack([jnp.sum(wide_fwd * wide_fwd, axis=1), jnp.sum(wide_bwd * wide_bwd, axis=1)])
    both = jnp.concatenate([scaled_bwd, scaled_fwd], axis=0)

    sibling = swap_core(both)
    far_bwd = [next_chip(scaled_bwd, d) for d in range(1, chips)]
    scales = lax.rsqrt(summed(squares) / full_width + EPS)
    scale_fwd, scale_bwd = scales[0][:, None], scales[1][:, None]
    near = project_near(near_ids, [both, sibling], w3)

    scaled_fwd, far_bwd, near = lax.optimization_barrier((scaled_fwd, far_bwd, near))
    far_bwd = [x for block in far_bwd for x in (block, swap_core(block))]
    far_fwd = [next_chip(scaled_fwd, d) for d in range(1, chips)]
    proj_bwd = project_far(far_ids, far_bwd, w3, near, 0, scale_bwd)
    grads, totals = attend_backward(block_lists[plan[0, 1]], proj_bwd, upstream, scale_bwd)
    totals = summed(jnp.sum(totals, axis=1))

    others = jnp.arange(chips, dtype=jnp.int32)
    theirs = grad_in_blocks(others * 2 + 1 - core, grads, w3, BF16)
    far_fwd, theirs, later = lax.optimization_barrier((far_fwd, theirs, grads))
    far_fwd = [x for block in far_fwd for x in (block, swap_core(block))]
    from_core = swap_core(theirs)
    target = [wrap(chip + d) for d in range(1, chips)]
    far_part = grad_in_blocks(jnp.stack([t * 2 + core for t in target]), later, w3, F32)
    sends = []
    for d in range(1, chips):
        here = lax.dynamic_index_in_dim(from_core, target[d - 1], 0, keepdims=False)
        sends.append((far_part[d - 1] + here.astype(F32)).astype(BF16))
    sends, later, from_core = lax.optimization_barrier((sends, later, from_core))
    arrived = [next_chip(block, d) for d, block in enumerate(sends, 1)]
    own_in = grad_in_blocks(me[None], later, w3, F32)[0]
    own_in, near = lax.optimization_barrier((own_in, near))
    own_in += lax.dynamic_index_in_dim(from_core, chip, 0, keepdims=False).astype(F32)

    proj_fwd = project_far(far_ids, far_fwd, w3, near, 1, scale_fwd)
    result = attend_forward(block_lists[plan[0, 0]], proj_fwd, forward_in)
    sent_on = shifted(result[None], "section", 1)

    for block in arrived:
        own_in += block.astype(F32)
    grad_x = upstream.astype(F32) + gain_row * own_in
    grad_x = grad_x - scale_bwd * (totals / full_width)[:, None] * wide_bwd
    sent_back = shifted(grad_x.astype(BF16)[None], "section", -1)
    grad_gain = jnp.sum(wide_bwd * own_in, axis=0)[None]
    all_ids = jnp.concatenate([near_ids, far_ids])
    grad_w = grad_weight(all_ids, [both, sibling, *far_bwd], grads)
    return (sent_on, sent_back, jnp.transpose(grad_w, (1, 0, 2))[None], grad_gain)


def solution(mesh):
    in_specs = (
        P("section", None, "fsdp"),
        P("section", None, "fsdp"),
        P("section", None, "fsdp"),
        P("section", None, None, "fsdp"),
        P("section", "fsdp"),
        P(),
        P("section", None),
    )
    out_specs = (
        P("section", None, "fsdp"),
        P("section", None, "fsdp"),
        P("section", None, None, "fsdp"),
        P("section", "fsdp"),
    )
    return jax.shard_map(
        on_device, mesh=mesh, in_specs=in_specs, out_specs=out_specs, check_vma=False
    )
```

```python
import functools
import math

import jax
import jax.numpy as jnp
from jax import lax
from jax.experimental import pallas as pl
from jax.experimental.pallas import tpu as pltpu
from jax.sharding import PartitionSpec as P

HD = 128
BLK = 128
EPS = 1e-05
INV = 1.0 / math.sqrt(HD)
LOG2E = math.log2(math.e)
VMEM = 28 * 1024 * 1024
F32 = jnp.float32
BF16 = jnp.bfloat16
NT = (((1,), (1,)), ((), ()))
TN = (((0,), (0,)), ((), ()))
TICK = jax.ShapeDtypeStruct((8, 128), jnp.int32)


def cost(flops, moved):
    return pl.CostEstimate(flops=flops // 1024, bytes_accessed=moved // 1024, transcendentals=0)


def params(*sem):
    return pltpu.CompilerParams(dimension_semantics=sem, vmem_limit_bytes=VMEM)


def total_of(x_refs, w_refs):
    total = jnp.dot(x_refs[0][...], w_refs[0][0], preferred_element_type=F32)
    for x_ref, w_ref in zip(x_refs[1:], w_refs[1:]):
        total += jnp.dot(x_ref[...], w_ref[0], preferred_element_type=F32)
    return total


def near_body(ids_ref, *refs):
    out_ref, tick_ref = refs[-2:]
    count = (len(refs) - 2) // 2
    tick_ref[...] = jnp.zeros_like(tick_ref)
    out_ref[0] = total_of(refs[:count], refs[count:-2]).astype(BF16)


def far_body(ids_ref, *refs):
    acc_ref, scale_ref, out_ref, tick_ref = refs[-4:]
    count = (len(refs) - 4) // 2
    tick_ref[...] = jnp.zeros_like(tick_ref)
    product = acc_ref[0].astype(F32) + total_of(refs[:count], refs[count:-4])
    out_ref[0] = (scale_ref[...] * product).astype(BF16)


def operand_specs(count, tokens, local, nt):
    specs = [pl.BlockSpec((tokens, local), lambda k, j, ids: (0, 0)) for _ in range(count)]
    for i in range(count):
        specs.append(pl.BlockSpec((1, local, nt), lambda k, j, ids, i=i: (k, ids[i], j)))
    return specs


def project_cost(tokens, count, local):
    return cost(6 * tokens * count * local * local, 6 * count * local * local)


def project_near(ids, blocks, w3):
    tokens, local = blocks[0].shape
    nt = min(256, local)
    count = len(blocks)
    return pl.pallas_call(
        near_body,
        grid_spec=pltpu.PrefetchScalarGridSpec(
            num_scalar_prefetch=1,
            grid=(3, local // nt),
            in_specs=operand_specs(count, tokens, local, nt),
            out_specs=[
                pl.BlockSpec((1, tokens, nt), lambda k, j, ids: (k, 0, j)),
                pl.BlockSpec((8, 128), lambda k, j, ids: (0, 0)),
            ],
        ),
        out_shape=[jax.ShapeDtypeStruct((3, tokens, local), BF16), TICK],
        compiler_params=params("arbitrary", "arbitrary"),
        cost_estimate=project_cost(tokens, count, local),
    )(ids, *blocks, *[w3] * count)


def project_far(ids, blocks, w3, acc, half, scale):
    tokens, local = blocks[0].shape
    nt = min(256, local)
    count = len(blocks)
    return pl.pallas_call(
        far_body,
        grid_spec=pltpu.PrefetchScalarGridSpec(
            num_scalar_prefetch=1,
            grid=(3, local // nt),
            in_specs=operand_specs(count, tokens, local, nt)
            + [
                pl.BlockSpec((1, tokens, nt), lambda k, j, ids: (k, half, j)),
                pl.BlockSpec((tokens, 1), lambda k, j, ids: (0, 0)),
            ],
            out_specs=[
                pl.BlockSpec((1, tokens, nt), lambda k, j, ids: (k, 0, j)),
                pl.BlockSpec((8, 128), lambda k, j, ids: (0, 0)),
            ],
        ),
        out_shape=[jax.ShapeDtypeStruct((3, tokens, local), BF16), TICK],
        compiler_params=params("arbitrary", "arbitrary"),
        cost_estimate=project_cost(tokens, count, local),
    )(ids, *blocks, *[w3] * count, acc, scale)


def scores_of(left_a, left_b, right):
    return (
        lax.dot_general(left_a, right, NT, preferred_element_type=F32),
        lax.dot_general(left_b, right, NT, preferred_element_type=F32),
    )


def probs_of(s_a, s_b):
    top = jnp.max(jnp.maximum(s_a, s_b), axis=0, keepdims=True)
    e_a = jnp.exp2((s_a - top) * (INV * LOG2E))
    e_b = jnp.exp2((s_b - top) * (INV * LOG2E))
    share = 1.0 / jnp.sum(e_a + e_b, axis=0, keepdims=True)
    return e_a * share, e_b * share


def units_of(ids_ref, tokens, cols):
    units = []
    for h in range(cols // HD):
        for b in range(tokens // BLK):
            other = pl.ds(pl.multiple_of(ids_ref[b, 1] * BLK, BLK), BLK)
            units.append((h, slice(h * HD, (h + 1) * HD), slice(b * BLK, (b + 1) * BLK), other))
    return units


def forward_body(ids_ref, q_ref, k_ref, v_ref, x_ref, out_ref):
    units = units_of(ids_ref, *x_ref.shape)
    scores = [
        scores_of(k_ref[0, bs, hs], k_ref[0, other, hs], q_ref[0, bs, hs])
        for _, hs, bs, other in units
    ]
    probs = [[p.astype(BF16) for p in probs_of(*pair)] for pair in scores]
    for (_, hs, bs, other), (p_a, p_b) in zip(units, probs):
        attn = lax.dot_general(p_a, v_ref[0, bs, hs], TN, preferred_element_type=F32)
        attn += lax.dot_general(p_b, v_ref[0, other, hs], TN, preferred_element_type=F32)
        out_ref[bs, hs] = (x_ref[bs, hs].astype(F32) + attn).astype(BF16)


def backward_body(ids_ref, q_ref, k_ref, v_ref, c_ref, scale_ref, grads_ref, total_ref, gk_ref, gv_ref):
    tokens, cols = c_ref.shape

    @pl.when(pl.program_id(0) == 0)
    def _():
        total_ref[...] = jnp.zeros_like(total_ref)

    units = units_of(ids_ref, tokens, cols)
    scores = [
        scores_of(k_ref[0, bs, hs], k_ref[0, other, hs], q_ref[0, bs, hs])
        for _, hs, bs, other in units
    ]
    grad_ps = [
        scores_of(v_ref[0, bs, hs], v_ref[0, other, hs], c_ref[bs, hs])
        for _, hs, bs, other in units
    ]
    lows = []
    for pair, (gp_a, gp_b) in zip(scores, grad_ps):
        p_a, p_b = probs_of(*pair)
        inner = jnp.sum(p_a * gp_a + p_b * gp_b, axis=0, keepdims=True)
        gs_a = (p_a * (gp_a - inner) * INV).astype(BF16)
        gs_b = (p_b * (gp_b - inner) * INV).astype(BF16)
        lows.append((p_a.astype(BF16), p_b.astype(BF16), gs_a, gs_b))
    later = []
    grad_qs = []
    for (h, hs, bs, other), (p_a, p_b, gs_a, gs_b) in zip(units, lows):
        q_b, c_b = q_ref[0, bs, hs], c_ref[bs, hs]
        gv_ref[h, bs, :] = jnp.dot(p_a, c_b, preferred_element_type=F32)
        gk_ref[h, bs, :] = jnp.dot(gs_a, q_b, preferred_element_type=F32)
        grad_q = lax.dot_general(gs_a, k_ref[0, bs, hs], TN, preferred_element_type=F32)
        grad_q += lax.dot_general(gs_b, k_ref[0, other, hs], TN, preferred_element_type=F32)
        grad_qs.append((scale_ref[bs, :] * grad_q).astype(BF16))
        later.append(
            (
                jnp.dot(p_b, c_b, preferred_element_type=F32),
                jnp.dot(gs_b, q_b, preferred_element_type=F32),
            )
        )
    for (h, _, _, other), (more_v, more_k) in zip(units, later):
        gv_ref[h, other, :] += more_v
        gk_ref[h, other, :] += more_k
    for (_, hs, bs, _), grad_q in zip(units, grad_qs):
        grads_ref[0, bs, hs] = grad_q
        total_ref[bs, :] += grad_q.astype(F32) * q_ref[0, bs, hs].astype(F32)
    for h in range(cols // HD):
        hs = slice(h * HD, (h + 1) * HD)
        grad_k = (scale_ref[...] * gk_ref[h]).astype(BF16)
        grad_v = (scale_ref[...] * gv_ref[h]).astype(BF16)
        grads_ref[1, :, hs] = grad_k
        grads_ref[2, :, hs] = grad_v
        total_ref[...] += grad_k.astype(F32) * k_ref[0, :, hs].astype(F32) + grad_v.astype(
            F32
        ) * v_ref[0, :, hs].astype(F32)


def attention_specs(tokens, hw):
    part = lambda k: pl.BlockSpec((1, tokens, hw), lambda h, ids: (k, 0, h))
    return [part(0), part(1), part(2), pl.BlockSpec((tokens, hw), lambda h, ids: (0, h))]


def attend_forward(ids, proj, x):
    tokens, local = x.shape
    hw = min(2 * HD, local)
    return pl.pallas_call(
        forward_body,
        grid_spec=pltpu.PrefetchScalarGridSpec(
            num_scalar_prefetch=1,
            grid=(local // hw,),
            in_specs=attention_specs(tokens, hw),
            out_specs=pl.BlockSpec((tokens, hw), lambda h, ids: (0, h)),
        ),
        out_shape=jax.ShapeDtypeStruct((tokens, local), BF16),
        compiler_params=params("arbitrary"),
        cost_estimate=cost(12 * tokens * tokens * local, 10 * tokens * local),
    )(ids, proj, proj, proj, x)


def attend_backward(ids, proj, c, scale):
    tokens, local = c.shape
    hw = min(2 * HD, local)
    return pl.pallas_call(
        backward_body,
        grid_spec=pltpu.PrefetchScalarGridSpec(
            num_scalar_prefetch=1,
            grid=(local // hw,),
            in_specs=attention_specs(tokens, hw)
            + [pl.BlockSpec((tokens, 1), lambda h, ids: (0, 0))],
            out_specs=[
                pl.BlockSpec((3, tokens, hw), lambda h, ids: (0, 0, h)),
                pl.BlockSpec((tokens, HD), lambda h, ids: (0, 0)),
            ],
            scratch_shapes=[pltpu.VMEM((hw // HD, tokens, HD), F32) for _ in range(2)],
        ),
        out_shape=[
            jax.ShapeDtypeStruct((3, tokens, local), BF16),
            jax.ShapeDtypeStruct((tokens, HD), F32),
        ],
        compiler_params=params("arbitrary"),
        cost_estimate=cost(24 * tokens * tokens * local, 14 * tokens * local),
    )(ids, proj, proj, proj, c, scale)


def grad_in_body(ids_ref, grads_ref, w_ref, out_ref):
    total = lax.dot_general(grads_ref[0], w_ref[0], NT, preferred_element_type=F32)
    for k in (1, 2):
        total += lax.dot_general(grads_ref[k], w_ref[k], NT, preferred_element_type=F32)
    out_ref[0] = total.astype(out_ref.dtype)


def grad_in_blocks(ids, grads, w3, out_type):
    tokens, local = grads.shape[1:]
    count = ids.shape[0]
    ft = min(512, local)
    steps = local // ft
    return pl.pallas_call(
        grad_in_body,
        grid_spec=pltpu.PrefetchScalarGridSpec(
            num_scalar_prefetch=1,
            grid=(count, steps),
            in_specs=[
                pl.BlockSpec((3, tokens, local), lambda i, j, ids: (0, 0, 0)),
                pl.BlockSpec((3, ft, local), lambda i, j, ids: (0, ids[i] * steps + j, 0)),
            ],
            out_specs=pl.BlockSpec((1, tokens, ft), lambda i, j, ids: (i, 0, j)),
        ),
        out_shape=jax.ShapeDtypeStruct((count, tokens, local), out_type),
        compiler_params=params("arbitrary", "arbitrary"),
        cost_estimate=cost(6 * tokens * count * local * local, 6 * count * local * local),
    )(ids, grads, w3)


def grad_w_body(count, ids_ref, *refs):
    grads_ref, out_ref = refs[-2:]
    for i, x_ref in enumerate(refs[-2 - count : -2]):

        @pl.when(pl.program_id(0) == i)
        def _():
            ft = out_ref.shape[1]
            start = pl.multiple_of(pl.program_id(1) * ft, ft)
            flipped = x_ref[:, pl.ds(start, ft)].T
            for k in range(3):
                out = jnp.dot(flipped, grads_ref[k], preferred_element_type=F32)
                out_ref[k] = out.astype(BF16)


def grad_weight(ids, blocks, grads, width, begun=()):
    _, tokens, local = grads.shape
    count = len(blocks)
    ft = min(512, local)
    steps = local // ft
    return pl.pallas_call(
        functools.partial(grad_w_body, count),
        grid_spec=pltpu.PrefetchScalarGridSpec(
            num_scalar_prefetch=1,
            grid=(count, steps),
            in_specs=[pl.BlockSpec(memory_space=pl.ANY) for _ in begun]
            + [pl.BlockSpec((tokens, local), lambda i, j, ids: (0, 0)) for _ in blocks]
            + [pl.BlockSpec((3, tokens, local), lambda i, j, ids: (0, 0, 0))],
            out_specs=pl.BlockSpec((3, ft, local), lambda i, j, ids: (0, ids[i] * steps + j, 0)),
        ),
        out_shape=jax.ShapeDtypeStruct((3, width, local), BF16),
        compiler_params=params("arbitrary", "arbitrary"),
        cost_estimate=project_cost(tokens, count, local),
        input_output_aliases={1: 0} if begun else {},
    )(ids, *begun, *blocks, grads)


def shifted(block, axis, distance):
    n = lax.axis_size(axis)
    return lax.ppermute(block, axis, [((i - distance) % n, i) for i in range(n)])


def swap_core(block):
    return lax.ppermute(block, "fsdp", [(i, i ^ 1) for i in range(lax.axis_size("fsdp"))])


def next_chip(block, distance):
    n = lax.axis_size("fsdp")
    route = [(i, ((i // 2 + distance) % (n // 2)) * 2 + i % 2) for i in range(n)]
    return lax.ppermute(block, "fsdp", route)


def all_parts(block):
    return [block] + [shifted(block, "fsdp", d) for d in range(1, lax.axis_size("fsdp"))]


def on_device(x_fwd, x_saved, cotangent, qkv_weight, gain, block_lists, plan):
    forward_in, saved_in, upstream = x_fwd[0], x_saved[0], cotangent[0]
    gain_row = gain[0][None, :]
    w3 = jnp.transpose(qkv_weight[0], (1, 0, 2))
    full_width, local = w3.shape[1:]
    tokens = forward_in.shape[0]
    n = lax.axis_size("fsdp")
    chips = n // 2
    me = lax.axis_index("fsdp").astype(jnp.int32)
    chip, core = lax.shift_right_logical(me, 1), me & 1
    wrap = lambda c: jnp.where(c < 0, c + chips, jnp.where(c >= chips, c - chips, c))
    near_ids = jnp.stack([me, me ^ 1])
    source = [wrap(chip - d) * 2 + core for d in range(1, chips)]
    far_ids = jnp.stack([i for s in source for i in (s, s ^ 1)])

    wide_fwd = forward_in.astype(F32)
    wide_bwd = saved_in.astype(F32)
    scaled_bwd = (wide_bwd * gain_row).astype(BF16)
    scaled_fwd = (wide_fwd * gain_row).astype(BF16)
    squares = jnp.stack([jnp.sum(wide_fwd * wide_fwd, axis=1), jnp.sum(wide_bwd * wide_bwd, axis=1)])
    both = jnp.concatenate([scaled_bwd, scaled_fwd], axis=0)

    sibling = swap_core(both)
    far_bwd = [next_chip(scaled_bwd, d) for d in range(1, chips)]
    scales = lax.rsqrt(sum(all_parts(squares)) / full_width + EPS)
    scale_fwd, scale_bwd = scales[0][:, None], scales[1][:, None]
    near, tick = project_near(near_ids, [both, sibling], w3)

    scaled_fwd, far_bwd, tick = lax.optimization_barrier((scaled_fwd, far_bwd, tick))
    far_ids = far_ids + tick[0, 0]
    far_bwd = [x for block in far_bwd for x in (block, swap_core(block))]
    far_fwd = [next_chip(scaled_fwd, d) for d in range(1, chips)]
    proj_bwd, _ = project_far(far_ids, far_bwd, w3, near, 0, scale_bwd)
    grads, totals = attend_backward(block_lists[plan[0, 1]], proj_bwd, upstream, scale_bwd)
    totals = all_parts(jnp.sum(totals, axis=1))

    others = jnp.arange(chips, dtype=jnp.int32)
    theirs = grad_in_blocks(others * 2 + 1 - core, grads, w3, BF16)
    far_fwd, theirs, later = lax.optimization_barrier((far_fwd, theirs, grads))
    far_fwd = [x for block in far_fwd for x in (block, swap_core(block))]
    from_core = swap_core(theirs)
    target = [wrap(chip + d) for d in range(1, chips)]
    far_part = grad_in_blocks(jnp.stack([t * 2 + core for t in target]), later, w3, F32)
    sends = []
    for d in range(1, chips):
        here = lax.dynamic_index_in_dim(from_core, target[d - 1], 0, keepdims=False)
        sends.append((far_part[d - 1] + here.astype(F32)).astype(BF16))
    sends, later, scale_fwd = lax.optimization_barrier((sends, later, scale_fwd))
    arrived = [next_chip(block, d) for d, block in enumerate(sends, 1)]
    own_in = grad_in_blocks(me[None], later, w3, F32)[0]
    own_in += lax.dynamic_index_in_dim(from_core, chip, 0, keepdims=False).astype(F32)

    proj_fwd, tick = project_far(far_ids, far_fwd, w3, near, 1, scale_fwd)
    arrived, totals, tick = lax.optimization_barrier((arrived, totals, tick))
    for block in arrived:
        own_in += block.astype(F32)
    grad_x = upstream.astype(F32) + gain_row * own_in
    grad_x = grad_x - scale_bwd * (sum(totals) / full_width)[:, None] * wide_bwd
    lists_fwd = block_lists[plan[0, 0]] + tick[0, 0]
    grad_x, lists_fwd = lax.optimization_barrier((grad_x.astype(BF16), lists_fwd))
    sent_back = shifted(grad_x[None], "section", -1)
    result = attend_forward(lists_fwd, proj_fwd, forward_in)
    grad_gain = jnp.sum(wide_bwd * own_in, axis=0)[None]
    begun = grad_weight(near_ids, [both, sibling], grads, full_width)
    sent_back, begun, result = lax.optimization_barrier((sent_back, begun, result))
    sent_on = shifted(result[None], "section", 1)
    grad_w = grad_weight(far_ids, far_bwd, grads, full_width, [begun])
    return (sent_on, sent_back, jnp.transpose(grad_w, (1, 0, 2))[None], grad_gain)


def solution(mesh):
    in_specs = (
        P("section", None, "fsdp"),
        P("section", None, "fsdp"),
        P("section", None, "fsdp"),
        P("section", None, None, "fsdp"),
        P("section", "fsdp"),
        P(),
        P("section", None),
    )
    out_specs = (
        P("section", None, "fsdp"),
        P("section", None, "fsdp"),
        P("section", None, None, "fsdp"),
        P("section", "fsdp"),
    )
    return jax.shard_map(
        on_device, mesh=mesh, in_specs=in_specs, out_specs=out_specs, check_vma=False
    )
```
